32 devices in a mesh: rows: 8 (over z, y), groups: 4 (over x, core).
Axes of the slice: x: 2, y: 2, z: 4, core: 2. Of those that a mesh axis runs over, the one named last changes fastest.
Arguments:
- snapshots: bfloat16 [16384, 1024], P('rows', 'groups'), may hold values from -6 to 6
- mass_diag: float32 [16384], P('rows'), may hold values from 0.5 to 2
- lower_coupling: float32 [8, 128, 128], P('rows'), may hold values from -0.5 to 0.5
- upper_coupling: float32 [8, 128, 128], P('rows'), may hold values from -0.5 to 0.5
- band_offsets: int32 [8, 2], P('rows'), may hold values from 1 to 2
- start_basis: float32 [1024, 512], replicated, may hold values from -6 to 6
Outputs:
- modes: float32 [16384, 512], P('rows', 'groups')
The draws below stay inside these ranges and needn't reach their ends.
All inputs are finite; a program needn't handle non-finite values.
Results may differ from the reference program's by a relative error of at most 0.0042.
Values may be sent and summed in bfloat16 or wider, within the bound.
A program may use at most 128 MiB of HBM per device.

```python
import math
import jax
import jax.numpy as jnp
from jax import lax

RB = 2048
NSNAP = 1024
MODES = 512
H = 128
ITERS = 3
NBLK = 8
NROWS = 16384


def with_ends(values, stream_key, low, top_value):
    longest = values.shape.index(max(values.shape))
    spots = []
    for shift in (0, 1):
        where = [jax.random.randint(jax.random.fold_in(stream_key, axis), (), 0, length) for axis, length in enumerate(values.shape)]
        where[longest] = (where[longest] + shift) % values.shape[longest]
        spots.append(tuple(where))
    return values.at[spots[0]].set(low).at[spots[1]].set(top_value)


def steps_of(own_key, dims, pieces, smallest, largest):
    def one(position, parts):
        steps = jax.random.uniform(jax.random.fold_in(jax.random.fold_in(own_key, 6), position), (parts,), jnp.float32, smallest / len(pieces), largest / len(pieces))
        return jnp.repeat(jnp.exp(steps), dims[position] // parts).reshape((-1,) + (1,) * (len(dims) - position - 1))

    factor_of = one(*pieces[0])
    for cut in pieces[1:]:
        factor_of = factor_of * one(*cut)
    return factor_of


def normal_values(stream_key, dims, width, limit, pieces=(), held_as=jnp.bfloat16):
    entries = jax.random.normal(stream_key, dims, jnp.float32) * width
    if len(pieces) > 0:
        entries = steps_of(stream_key, dims, pieces, -0.22, 0.18) * entries
    return jnp.clip(entries, min=-limit, max=limit).astype(held_as)


def setup_inputs(seed: int = 0) -> dict:
    splits = jax.random.split(jax.random.key(seed), 7)
    return {
        "snapshots": normal_values(splits[0], (NROWS, NSNAP), 1.0, 6.0, ((0, 8), (1, 4))),
        "mass_diag": jnp.clip(jnp.exp(math.log(2.0) - 1.3862944 * jax.random.uniform(splits[1], (NROWS,), jnp.float32) ** steps_of(splits[1], (NROWS,), ((0, 8),), -0.2, 0.2)), 0.5, 2.0),
        "lower_coupling": normal_values(splits[2], (NBLK, H, H), H ** -0.5, 0.5, ((0, 8),), jnp.float32),
        "upper_coupling": normal_values(splits[3], (NBLK, H, H), H ** -0.5, 0.5, ((0, 8),), jnp.float32),
        "band_offsets": with_ends(jax.random.randint(splits[4], (NBLK, 2), 1, 3), jax.random.fold_in(splits[4], 1), 1, 2).astype(jnp.int32),
        "start_basis": normal_values(splits[5], (NSNAP, MODES), 1.0, 6.0, (), jnp.float32),
    }


def orthonormal(image):
    correlation = jnp.dot(image.T.astype(jnp.float32), image.astype(jnp.float32), precision=lax.Precision.HIGHEST, preferred_element_type=jnp.float32)
    lower = jnp.linalg.cholesky(correlation)
    return lax.linalg.triangular_solve(lower, image, left_side=False, lower=True, transpose_a=True)

def reference(snapshots, mass_diag, lower_coupling, upper_coupling, band_offsets, start_basis):
    blocks = snapshots.reshape(NBLK, RB, NSNAP)
    bottom = blocks[:, RB - H:, :].astype(jnp.float32)
    top = blocks[:, :H, :].astype(jnp.float32)
    block_ids = jnp.arange(NBLK, dtype=jnp.int32)
    lower_ids = block_ids - band_offsets[:, 0]
    upper_ids = block_ids + band_offsets[:, 1]
    lower_ok = (lower_ids >= 0).astype(jnp.float32)[:, None, None]
    upper_ok = (upper_ids < NBLK).astype(jnp.float32)[:, None, None]
    lower_rims = bottom[jnp.clip(lower_ids, 0, NBLK - 1)] * lower_ok
    upper_rims = top[jnp.clip(upper_ids, 0, NBLK - 1)] * upper_ok
    lower_terms = jnp.einsum('ihk,iks->ihs', lower_coupling, lower_rims, precision=lax.Precision.HIGHEST)
    upper_terms = jnp.einsum('ihk,iks->ihs', upper_coupling, upper_rims, precision=lax.Precision.HIGHEST)
    weighted = mass_diag.reshape(NBLK, RB, 1) * blocks.astype(jnp.float32)
    weighted = weighted.at[:, :H, :].add(lower_terms)
    weighted = weighted.at[:, RB - H:, :].add(upper_terms)
    weighted = weighted.reshape(NROWS, NSNAP).astype(jnp.bfloat16)
    gram = jnp.dot(weighted.T.astype(jnp.float32), weighted.astype(jnp.float32), preferred_element_type=jnp.float32) / NROWS
    basis = start_basis
    for turn_index in range(ITERS):
        image = jnp.dot(gram.astype(jnp.float32), basis.astype(jnp.float32), precision=lax.Precision.HIGHEST, preferred_element_type=jnp.float32)
        basis = orthonormal(image)
    basis_low = basis.astype(jnp.bfloat16)
    return jnp.dot(weighted.astype(jnp.float32), basis_low.astype(jnp.float32), preferred_element_type=jnp.float32)
```

```python
import functools

import jax
import jax.numpy as jnp
from jax import lax
from jax.experimental import pallas as pl
from jax.experimental.pallas import tpu as pltpu
from jax.sharding import PartitionSpec as P

ITERS = 3
BF16 = jnp.bfloat16
F32 = jnp.float32

LOOSE = 0.04
TIGHT = 0.003
REFINED = 1e-4
MOST_STEPS = 14


def dot_nn(a, b):
    return lax.dot_general(a, b, (((1,), (0,)), ((), ())), preferred_element_type=F32)


def dot_nt(a, b):
    return lax.dot_general(a, b, (((1,), (1,)), ((), ())), preferred_element_type=F32)


def split(value):
    high = value.astype(BF16)
    return high, (value - high.astype(F32)).astype(BF16)


def ids(shape):
    return lax.broadcasted_iota(jnp.int32, shape, 0), lax.broadcasted_iota(jnp.int32, shape, 1)


def half_lower(residual):
    row, col = ids(residual.shape)
    return jnp.where(row > col, residual, jnp.where(row == col, 0.5 * residual, 0.0))


def minus_identity(product):
    row, col = ids(product.shape)
    return product - jnp.where(row == col, 1.0, 0.0)


def triangular_inverse(corr, limit, corr_ref, x_ref):
    modes = corr.shape[0]
    row, col = ids(corr.shape)
    diagonal = jnp.where(row == col, corr, 0.0)
    scale_rows = lax.rsqrt(jnp.sum(diagonal, axis=1, keepdims=True))
    scale_cols = lax.rsqrt(jnp.sum(diagonal, axis=0, keepdims=True))
    scaled = corr * scale_rows * scale_cols
    corr_ref[...] = scaled.astype(BF16)
    x_ref[...] = jnp.where(row > col, -scaled, jnp.where(row == col, 1.0, 0.0)).astype(BF16)

    def more(state):
        return (state[0] < MOST_STEPS) & (state[1] > limit * modes)

    def step(state):
        x = x_ref[...]
        half = dot_nn(x, corr_ref[...]).astype(BF16)
        residual = minus_identity(dot_nt(half, x))
        size = jnp.sum(residual * residual)
        change = dot_nn(half_lower(residual).astype(BF16), x)
        x_ref[...] = (x.astype(F32) - change).astype(BF16)
        return state[0] + 1, size

    _, size = lax.while_loop(more, step, (jnp.int32(0), jnp.float32(jnp.inf)))
    x = x_ref[...].astype(F32)
    smallest = jnp.min(jnp.where(row == col, x, 1.0))
    x_ref[...] = (x * scale_cols).astype(BF16)
    return (size <= limit * modes) & (smallest > 0.0)


def start_kernel(start_ref, high_ref, low_ref, ok_ref, corr_ref, x_ref):
    high, low = split(start_ref[...])
    ok = triangular_inverse(dot_nt(high, high), LOOSE, corr_ref, x_ref)
    x = x_ref[...]
    high_ref[...], low_ref[...] = split(dot_nn(x, high) + dot_nn(x, low))
    ok_ref[0] = ok.astype(jnp.int32)


def iterate_kernel(
    part_ref, gram_ref, high_in, low_in, basis_ref, ok_ref, gram_high, gram_low, image, high, low, corr_ref, x_ref, e_ref
):
    modes, snaps = image.shape
    tile = 256
    part_modes = basis_ref.shape[0]

    def split_gram(step, carry):
        rows = pl.ds(pl.multiple_of(step * tile, tile), tile)
        gram_high[rows, :], gram_low[rows, :] = split(gram_ref[rows, :])
        return carry

    lax.fori_loop(0, snaps // tile, split_gram, 0)
    high[...] = high_in[...]
    low[...] = low_in[...]
    ok = jnp.bool_(True)
    for turn in range(ITERS):

        def multiply(step, carry):
            cols = pl.ds(pl.multiple_of(step * tile, tile), tile)
            g = gram_high[:, cols]
            image[:, cols] = dot_nn(high[...], g) + (dot_nn(high[...], gram_low[:, cols]) + dot_nn(low[...], g))
            return carry

        lax.fori_loop(0, snaps // tile, multiply, 0)
        high[...], low[...] = split(image[...])
        limit = TIGHT if turn == ITERS - 1 else LOOSE
        ok = ok & triangular_inverse(dot_nt(high[...], high[...]), limit, corr_ref, x_ref)

        def apply(step, carry):
            cols = pl.ds(pl.multiple_of(step * tile, tile), tile)
            x = x_ref[...]
            image[:, cols] = dot_nn(x, high[:, cols]) + dot_nn(x, low[:, cols])
            return carry

        lax.fori_loop(0, snaps // tile, apply, 0)
        high[...], low[...] = split(image[...])

    def more(state):
        return (state[0] < 4) & (state[1] > REFINED * modes)

    def refine(state):
        cross = dot_nt(high[...], low[...])
        residual = minus_identity(dot_nt(high[...], high[...]) + (cross + dot_nt(low[...], high[...])))
        size = jnp.sum(residual * residual)
        e_ref[...] = half_lower(residual).astype(BF16)

        @pl.when(size > REFINED * modes)
        def _():
            image[...] = image[...] - dot_nn(e_ref[...], high[...])
            high[...], low[...] = split(image[...])

        return state[0] + 1, size

    _, size = lax.while_loop(more, refine, (jnp.int32(0), jnp.float32(jnp.inf)))
    rows = pl.ds(pl.multiple_of(part_ref[0] * part_modes, part_modes), part_modes)
    basis_ref[...] = (image[rows, :] - dot_nn(e_ref[rows, :], high[...])).astype(BF16)
    ok_ref[0] = (ok & (size <= REFINED * modes)).astype(jnp.int32)


VMEM = pl.BlockSpec(memory_space=pltpu.VMEM)
SMEM = pl.BlockSpec(memory_space=pltpu.SMEM)
LIMIT = 56 * 2**20


def prepare_start(start_basis):
    snaps, modes = start_basis.shape
    return pl.pallas_call(
        start_kernel,
        name="prepare_start",
        out_shape=(
            jax.ShapeDtypeStruct((modes, snaps), BF16),
            jax.ShapeDtypeStruct((modes, snaps), BF16),
            jax.ShapeDtypeStruct((1,), jnp.int32),
        ),
        in_specs=[VMEM],
        out_specs=(VMEM, VMEM, SMEM),
        scratch_shapes=[pltpu.VMEM((modes, modes), BF16), pltpu.VMEM((modes, modes), BF16)],
        compiler_params=pltpu.CompilerParams(vmem_limit_bytes=LIMIT),
        cost_estimate=pl.CostEstimate(flops=30 * modes**3, bytes_accessed=4 * snaps * modes, transcendentals=0),
    )(start_basis.T)


def iterate(part, part_modes, gram, high, low):
    modes, snaps = high.shape
    return pl.pallas_call(
        iterate_kernel,
        name="iterate",
        out_shape=(jax.ShapeDtypeStruct((part_modes, snaps), BF16), jax.ShapeDtypeStruct((1,), jnp.int32)),
        in_specs=[SMEM, VMEM, VMEM, VMEM],
        out_specs=(VMEM, SMEM),
        scratch_shapes=[
            pltpu.VMEM((snaps, snaps), BF16),
            pltpu.VMEM((snaps, snaps), BF16),
            pltpu.VMEM((modes, snaps), F32),
            pltpu.VMEM((modes, snaps), BF16),
            pltpu.VMEM((modes, snaps), BF16),
            pltpu.VMEM((modes, modes), BF16),
            pltpu.VMEM((modes, modes), BF16),
            pltpu.VMEM((modes, modes), BF16),
        ],
        compiler_params=pltpu.CompilerParams(vmem_limit_bytes=LIMIT),
        cost_estimate=pl.CostEstimate(flops=150 * modes**3, bytes_accessed=4 * snaps * snaps, transcendentals=0),
    )(part, gram, high, low)


def orthonormal(image):
    correlation = jnp.dot(image.T, image, precision=lax.Precision.HIGHEST, preferred_element_type=F32)
    lower = jnp.linalg.cholesky(correlation)
    return lax.linalg.triangular_solve(lower, image, left_side=False, lower=True, transpose_a=True)


def direct_part(group_index, part_modes, gram, start_basis):
    basis = start_basis
    for _ in range(ITERS):
        image = jnp.dot(gram, basis, precision=lax.Precision.HIGHEST, preferred_element_type=F32)
        basis = orthonormal(image)
    return lax.dynamic_slice_in_dim(basis.astype(BF16).T, group_index * part_modes, part_modes, 0)


def from_behind(value, axis, by):
    devices = lax.axis_size(axis)
    pairs = [(i, i + by) for i in range(devices) if 0 <= i + by < devices]
    return lax.ppermute(value, axis, pairs)


def rim_terms(coupling, rims):
    return jnp.dot(coupling, rims, precision=lax.Precision.HIGHEST, preferred_element_type=F32)


def shards(snapshots, mass_diag, lower_coupling, upper_coupling, band_offsets, start_basis):
    block_rows = snapshots.shape[0]
    rim_rows = lower_coupling.shape[1]
    total_rows = block_rows * lax.axis_size("rows")
    bottom_rim = snapshots[block_rows - rim_rows :, :]
    top_rim = snapshots[:rim_rows, :]
    below_one, below_two = (from_behind(bottom_rim, "rows", by) for by in (1, 2))
    above_one, above_two = (from_behind(top_rim, "rows", -by) for by in (1, 2))
    lower_rims = jnp.where(band_offsets[0, 0] == 1, below_one, below_two).astype(F32)
    upper_rims = jnp.where(band_offsets[0, 1] == 1, above_one, above_two).astype(F32)
    weighted = mass_diag[:, None] * snapshots.astype(F32)
    weighted = weighted.at[:rim_rows, :].add(rim_terms(lower_coupling[0], lower_rims))
    weighted = weighted.at[block_rows - rim_rows :, :].add(rim_terms(upper_coupling[0], upper_rims))
    weighted = weighted.astype(BF16)
    gathered = lax.all_gather(weighted, "groups", axis=1, tiled=True)
    gram_rows = lax.dot_general(weighted, gathered, (((0,), (0,)), ((), ())), preferred_element_type=F32)
    gram_rows = lax.psum(gram_rows, "rows") / total_rows
    gram = lax.all_gather(gram_rows, "groups", axis=0, tiled=True)
    group_index = lax.axis_index("groups")
    part_modes = start_basis.shape[1] // lax.axis_size("groups")
    high, low, start_ok = prepare_start(start_basis)
    basis_part, iterate_ok = iterate(group_index.reshape(1), part_modes, gram, high, low)
    basis_part = lax.cond(
        (start_ok[0] > 0) & (iterate_ok[0] > 0),
        lambda *_: basis_part,
        functools.partial(direct_part, group_index, part_modes),
        gram,
        start_basis,
    )
    return lax.dot_general(gathered, basis_part, (((1,), (1,)), ((), ())), preferred_element_type=F32)


def solution(mesh):
    placed = (
        P("rows", "groups"),
        P("rows"),
        P("rows", None, None),
        P("rows", None, None),
        P("rows", None),
        P(),
    )
    return jax.shard_map(
        shards, mesh=mesh, in_specs=placed, out_specs=P("rows", "groups"), check_vma=False
    )
```

```python
import functools

import jax
import jax.numpy as jnp
from jax import lax
from jax.experimental import pallas as pl
from jax.experimental.pallas import tpu as pltpu
from jax.sharding import PartitionSpec as P

ITERS = 3
BF16 = jnp.bfloat16
F32 = jnp.float32

LOOSE = 0.04
TIGHT = 0.003
REFINED = 1e-4
MOST_STEPS = 14


def dot_nn(a, b):
    return lax.dot_general(a, b, (((1,), (0,)), ((), ())), preferred_element_type=F32)


def dot_nt(a, b):
    return lax.dot_general(a, b, (((1,), (1,)), ((), ())), preferred_element_type=F32)


def split(value):
    high = value.astype(BF16)
    return high, (value - high.astype(F32)).astype(BF16)


def ids(shape):
    return lax.broadcasted_iota(jnp.int32, shape, 0), lax.broadcasted_iota(jnp.int32, shape, 1)


def half_lower(residual):
    row, col = ids(residual.shape)
    return jnp.where(row > col, residual, jnp.where(row == col, 0.5 * residual, 0.0))


def minus_identity(product):
    row, col = ids(product.shape)
    return product - jnp.where(row == col, 1.0, 0.0)


def triangular_inverse(corr, limit, corr_ref, x_ref):
    modes = corr.shape[0]
    row, col = ids(corr.shape)
    diagonal = jnp.where(row == col, corr, 0.0)
    scale_rows = lax.rsqrt(jnp.sum(diagonal, axis=1, keepdims=True))
    scale_cols = lax.rsqrt(jnp.sum(diagonal, axis=0, keepdims=True))
    scaled = corr * scale_rows * scale_cols
    corr_ref[...] = scaled.astype(BF16)
    x_ref[...] = jnp.where(row > col, -scaled, jnp.where(row == col, 1.0, 0.0)).astype(BF16)

    def more(state):
        return (state[0] < MOST_STEPS) & (state[1] > limit * modes)

    def step(state):
        x = x_ref[...]
        half = dot_nn(x, corr_ref[...]).astype(BF16)
        residual = minus_identity(dot_nt(half, x))
        size = jnp.sum(residual * residual)
        change = dot_nn(half_lower(residual).astype(BF16), x)
        x_ref[...] = (x.astype(F32) - change).astype(BF16)
        return state[0] + 1, size

    _, size = lax.while_loop(more, step, (jnp.int32(0), jnp.float32(jnp.inf)))
    x = x_ref[...].astype(F32)
    smallest = jnp.min(jnp.where(row == col, x, 1.0))
    x_ref[...] = (x * scale_cols).astype(BF16)
    return (size <= limit * modes) & (smallest > 0.0)


def start_kernel(start_ref, high_ref, low_ref, ok_ref, corr_ref, x_ref):
    high, low = split(start_ref[...])
    ok = triangular_inverse(dot_nt(high, high), LOOSE, corr_ref, x_ref)
    x = x_ref[...]
    high_ref[...], low_ref[...] = split(dot_nn(x, high) + dot_nn(x, low))
    ok_ref[0] = ok.astype(jnp.int32)


def iterate_kernel(
    second_rows, part_ref, gram_ref, high_in, low_in, basis_ref, ok_ref, gram_high, gram_low, image, high, low, corr_ref, x_ref, e_ref
):
    modes, snaps = image.shape
    tile = 256
    part_modes = basis_ref.shape[0]

    width = gram_ref.shape[-1]
    quarter, half = width // 4, width // 2
    first = gram_ref.shape[3] - second_rows

    def place(row, col, block):
        rows, cols = block.shape
        gram_high[row : row + rows, col : col + cols], gram_low[row : row + rows, col : col + cols] = split(block)

    for x in range(2):
        for c in range(2):
            corner = (2 * x + c) * width
            place(corner, corner, gram_ref[x, c, 0, : 3 * quarter, :])
            place(corner + 3 * quarter, corner, gram_ref[x, c, 1, :quarter, :])
            side = gram_ref[x, c, 1, quarter : 3 * quarter, :]
            place(2 * x * width + c * half, (2 * x + 1) * width, side)
            place((2 * x + 1) * width, 2 * x * width + c * half, side.T)
            for y in range(2):
                cross = gram_ref[x, c, y, first : first + half, :]
                place(c * width + y * half, (2 + x) * width, cross)
                place((2 + x) * width, c * width + y * half, cross.T)
    high[...] = high_in[...]
    low[...] = low_in[...]
    ok = jnp.bool_(True)
    for turn in range(ITERS):

        def multiply(step, carry):
            cols = pl.ds(pl.multiple_of(step * tile, tile), tile)
            g = gram_high[:, cols]
            image[:, cols] = dot_nn(high[...], g) + (dot_nn(high[...], gram_low[:, cols]) + dot_nn(low[...], g))
            return carry

        lax.fori_loop(0, snaps // tile, multiply, 0)
        high[...], low[...] = split(image[...])
        limit = TIGHT if turn == ITERS - 1 else LOOSE
        ok = ok & triangular_inverse(dot_nt(high[...], high[...]), limit, corr_ref, x_ref)

        def apply(step, carry):
            cols = pl.ds(pl.multiple_of(step * tile, tile), tile)
            x = x_ref[...]
            image[:, cols] = dot_nn(x, high[:, cols]) + dot_nn(x, low[:, cols])
            return carry

        lax.fori_loop(0, snaps // tile, apply, 0)
        high[...], low[...] = split(image[...])

    def more(state):
        return (state[0] < 4) & (state[1] > REFINED * modes)

    def refine(state):
        cross = dot_nt(high[...], low[...])
        residual = minus_identity(dot_nt(high[...], high[...]) + (cross + dot_nt(low[...], high[...])))
        size = jnp.sum(residual * residual)
        e_ref[...] = half_lower(residual).astype(BF16)

        @pl.when(size > REFINED * modes)
        def _():
            image[...] = image[...] - dot_nn(e_ref[...], high[...])
            high[...], low[...] = split(image[...])

        return state[0] + 1, size

    _, size = lax.while_loop(more, refine, (jnp.int32(0), jnp.float32(jnp.inf)))
    rows = pl.ds(pl.multiple_of(part_ref[0] * part_modes, part_modes), part_modes)
    basis_ref[...] = (image[rows, :] - dot_nn(e_ref[rows, :], high[...])).astype(BF16)
    ok_ref[0] = (ok & (size <= REFINED * modes)).astype(jnp.int32)


VMEM = pl.BlockSpec(memory_space=pltpu.VMEM)
SMEM = pl.BlockSpec(memory_space=pltpu.SMEM)
LIMIT = 56 * 2**20


def prepare_start(start_basis):
    snaps, modes = start_basis.shape
    return pl.pallas_call(
        start_kernel,
        name="prepare_start",
        out_shape=(
            jax.ShapeDtypeStruct((modes, snaps), BF16),
            jax.ShapeDtypeStruct((modes, snaps), BF16),
            jax.ShapeDtypeStruct((1,), jnp.int32),
        ),
        in_specs=[VMEM],
        out_specs=(VMEM, VMEM, SMEM),
        scratch_shapes=[pltpu.VMEM((modes, modes), BF16), pltpu.VMEM((modes, modes), BF16)],
        compiler_params=pltpu.CompilerParams(vmem_limit_bytes=LIMIT),
        cost_estimate=pl.CostEstimate(flops=30 * modes**3, bytes_accessed=4 * snaps * modes, transcendentals=0),
    )(start_basis.T)


def iterate(part, part_modes, second_rows, gram, high, low):
    modes, snaps = high.shape
    return pl.pallas_call(
        functools.partial(iterate_kernel, second_rows),
        name="iterate",
        out_shape=(jax.ShapeDtypeStruct((part_modes, snaps), BF16), jax.ShapeDtypeStruct((1,), jnp.int32)),
        in_specs=[SMEM, VMEM, VMEM, VMEM],
        out_specs=(VMEM, SMEM),
        scratch_shapes=[
            pltpu.VMEM((snaps, snaps), BF16),
            pltpu.VMEM((snaps, snaps), BF16),
            pltpu.VMEM((modes, snaps), F32),
            pltpu.VMEM((modes, snaps), BF16),
            pltpu.VMEM((modes, snaps), BF16),
            pltpu.VMEM((modes, modes), BF16),
            pltpu.VMEM((modes, modes), BF16),
            pltpu.VMEM((modes, modes), BF16),
        ],
        compiler_params=pltpu.CompilerParams(vmem_limit_bytes=LIMIT),
        cost_estimate=pl.CostEstimate(flops=150 * modes**3, bytes_accessed=4 * snaps * snaps, transcendentals=0),
    )(part, gram, high, low)


def orthonormal(image):
    correlation = jnp.dot(image.T, image, precision=lax.Precision.HIGHEST, preferred_element_type=F32)
    lower = jnp.linalg.cholesky(correlation)
    return lax.linalg.triangular_solve(lower, image, left_side=False, lower=True, transpose_a=True)


def direct_part(group_index, part_modes, gram, start_basis):
    basis = start_basis
    for _ in range(ITERS):
        image = jnp.dot(gram, basis, precision=lax.Precision.HIGHEST, preferred_element_type=F32)
        basis = orthonormal(image)
    return lax.dynamic_slice_in_dim(basis.astype(BF16).T, group_index * part_modes, part_modes, 0)


def dot_tn(a, b):
    return lax.dot_general(a, b, (((0,), (0,)), ((), ())), preferred_element_type=F32)


def rim_terms(coupling, rims):
    high, rest = split(coupling)
    middle = (coupling - high.astype(F32)).astype(BF16)
    low = (coupling - high.astype(F32) - middle.astype(F32)).astype(BF16)
    return dot_nn(high, rims) + (dot_nn(middle, rims) + dot_nn(low, rims))


class Layout:
    def __init__(self, devices, width):
        self.depth = devices // 2
        up = lambda rows: -(-rows // (8 * self.depth)) * 8
        self.chunks = (up(width * 3 // 4), up(width // 2))
        self.halves = tuple(chunk * self.depth for chunk in self.chunks)


def exchange_kernel(
    lay, base_ref, rims_ref, top_ref, bottom_ref, lower_ref, upper_ref, pick_ref, wall_out, gram_out,
    wall, rims_in, part, cross, cross_in, y_in0, y_in1, h0, h1, z_in0, z_in1, pieces, send_sem, recv_sem, out_sem,
):
    devices, depth = lax.axis_size("rows"), lay.depth
    me, group = lax.axis_index("rows"), lax.axis_index("groups")
    z, y, x, c = me // 2, me % 2, group // 2, group % 2
    block_rows, width = base_ref.shape
    rim = top_ref.shape[0]
    middle_rows, half_rows = block_rows - 2 * rim, block_rows // 2
    core_peer, x_peer = (me, 2 * x + 1 - c), (me, 2 * (1 - x) + c)
    y_peer = (2 * z + 1 - y, group)
    z_peers = [(2 * lax.rem(z + d, depth) + y, group) for d in range(1, depth)]
    rim_peers = [(lax.rem(me + d + devices, devices), group) for d in (1, 2, -1, -2)]
    peers = [core_peer, x_peer, y_peer] + z_peers + rim_peers

    started = []

    def send(src, dst, peer):
        k = len(started)
        copy = pltpu.make_async_remote_copy(
            src_ref=src, dst_ref=dst, send_sem=send_sem.at[k], recv_sem=recv_sem.at[k],
            device_id=peer, device_id_type=pl.DeviceIdType.MESH,
        )
        copy.start()
        started.append(copy)
        return copy

    def part_of(ref, row, rows, col=None):
        rows = pl.ds(pl.multiple_of(row, 8), rows)
        return ref.at[rows, :] if col is None else ref.at[rows, pl.ds(pl.multiple_of(col * width, width), width)]

    barrier = pltpu.get_barrier_semaphore()
    for peer in peers:
        pl.semaphore_signal(barrier, inc=1, device_id=peer, device_id_type=pl.DeviceIdType.MESH)
    pl.semaphore_wait(barrier, len(peers))

    rim_copies = [
        send(src, rims_in.at[k], peer)
        for k, (src, peer) in enumerate(zip((bottom_ref, bottom_ref, top_ref, top_ref), rim_peers))
    ]
    there = 1 - x
    inner = rim + there * (half_rows - rim)
    outer = there * (block_rows - rim)
    to_x = [send(part_of(base_ref, inner, half_rows - rim), part_of(wall, inner, half_rows - rim, group), x_peer)]
    to_core = [send(part_of(base_ref, rim, middle_rows), part_of(wall, rim, middle_rows, group), core_peer)]
    mine = pl.ds(pl.multiple_of(group * width, width), width)
    wall[rim : block_rows - rim, mine] = base_ref[rim : block_rows - rim, :]
    for copy in rim_copies:
        copy.wait_recv()
    below = rims_in[0].astype(F32) * pick_ref[0] + rims_in[1].astype(F32) * pick_ref[1]
    above = rims_in[2].astype(F32) * pick_ref[2] + rims_in[3].astype(F32) * pick_ref[3]
    wall[:rim, mine] = (rims_ref[:rim, :] + rim_terms(lower_ref[...], below.astype(BF16))).astype(BF16)
    wall[block_rows - rim :, mine] = (rims_ref[rim:, :] + rim_terms(upper_ref[...], above.astype(BF16))).astype(BF16)
    to_x.append(send(part_of(wall, outer, rim, group), part_of(wall, outer, rim, group), x_peer))
    for row in (0, block_rows - rim):
        to_core.append(send(part_of(wall, row, rim, group), part_of(wall, row, rim, group), core_peer))

    quarter, half = width // 4, width // 2
    first, second = lay.halves
    if first + second > 5 * quarter:
        part[...] = jnp.zeros_like(part)
    own = wall[:, mine]
    diagonal = dot_tn(own, own)
    part[0, : 3 * quarter, :] = diagonal[: 3 * quarter, :]
    part[1, :quarter, :] = diagonal[3 * quarter :, :]
    for copy in to_core:
        copy.wait_recv()
    left = pl.ds(pl.multiple_of(2 * x * width + c * half, half), half)
    right = pl.ds(pl.multiple_of((2 * x + 1) * width, width), width)
    part[1, quarter : 3 * quarter, :] = dot_tn(wall[:, left], wall[:, right])

    total_rows = block_rows * devices

    def window(ref, k, row, rows):
        return ref.at[k, pl.ds(pl.multiple_of(row, 8), rows), :]

    def segment(k):
        rows, chunk, start = lay.halves[k], lay.chunks[k], k * first
        y_in, h, z_in = (y_in0, h0, z_in0) if k == 0 else (y_in1, h1, z_in1)

        def piece(xs, cs, ys, row, count):
            return pieces.at[xs, cs, ys, pl.ds(pl.multiple_of(start + row, 8), count), :]

        def same(xs, ys, row, count, peer):
            return send(piece(xs, c, ys, row, count), piece(xs, c, ys, row, count), peer)

        copy = send(window(part, 1 - y, start, rows), y_in, y_peer)
        yield
        copy.wait_recv()
        h[...] = part[y, start : start + rows, :] + y_in[...]
        copies = []
        for d in range(1, depth):
            there = lax.rem(z + d, depth)
            copies.append(send(part_of(h, there * chunk, chunk), z_in.at[d - 1], z_peers[d - 1]))
        yield
        for copy in copies:
            copy.wait_recv()
        own = h[pl.ds(pl.multiple_of(z * chunk, 8), chunk), :]
        for d in range(1, depth):
            own = own + z_in[d - 1]
        pieces[x, c, y, pl.ds(pl.multiple_of(start + z * chunk, 8), chunk), :] = own / total_rows
        copies = [same(x, y, z * chunk, chunk, peer) for peer in z_peers]
        yield
        for copy in copies:
            copy.wait_recv()
        from_y = same(x, y, 0, rows, y_peer)
        last = [same(x, y, 0, rows, core_peer)]
        yield
        from_x = same(x, y, 0, rows, x_peer)
        yield
        from_y.wait_recv()
        part_x = same(x, 1 - y, 0, rows // 2, x_peer)
        last.append(same(x, 1 - y, 0, rows, core_peer))
        from_x.wait_recv()
        part_y = same(1 - x, y, rows // 2, rows // 2, y_peer)
        last.append(same(1 - x, y, 0, rows, core_peer))
        yield
        part_x.wait_recv()
        part_y.wait_recv()
        last.append(same(1 - x, 1 - y, 0, rows, core_peer))
        yield
        for copy in last:
            copy.wait_recv()
        yield

    chip = segment(0)
    next(chip)
    next(chip)
    next(chip)
    for copy in to_x:
        copy.wait_recv()
    here = x * half_rows
    other = 2 * (1 - x) + c
    relay = send(part_of(wall, here, half_rows, other), part_of(wall, here, half_rows, other), core_peer)
    relay.wait_recv()
    rows = pl.ds(pl.multiple_of(here, half_rows), half_rows)
    factor = wall[rows, pl.ds(pl.multiple_of(c * width, width), width)]
    for side in range(2):
        cross[side] = dot_tn(factor, wall[rows, (2 + side) * width : (3 + side) * width])
    to_cross = send(cross.at[1 - x], cross_in, x_peer)
    next(chip)
    to_cross.wait_recv()
    total = cross[x] + cross_in[...]
    part[0, first : first + half, :] = total[:half, :]
    part[1, first : first + half, :] = total[half:, :]
    across = segment(1)
    next(across)
    next(chip)
    next(across)
    next(chip)
    rest = send(part_of(wall, here, half_rows, group), part_of(wall, here, half_rows, group), x_peer)
    next(across)
    next(chip)
    next(across)
    next(across)
    next(chip)
    next(across)
    rest.wait_recv()
    far = there * half_rows
    relay = send(part_of(wall, far, half_rows, other), part_of(wall, far, half_rows, other), core_peer)
    next(across)
    relay.wait_recv()
    wall_copy = pltpu.make_async_copy(wall, wall_out, out_sem.at[0])
    wall_copy.start()
    next(across)
    gram_copy = pltpu.make_async_copy(pieces, gram_out, out_sem.at[1])
    gram_copy.start()
    for copy in started:
        copy.wait_send()
    wall_copy.wait()
    gram_copy.wait()


def exchange(lay, base, rims, top, bottom, lower, upper, pick):
    block_rows, width = base.shape
    rim = top.shape[0]
    first, second = lay.halves
    depth = lay.depth
    copies = 13 + 2 * (9 + 2 * (depth - 1))
    pieces = (2, 2, 2, first + second, width)
    return pl.pallas_call(
        functools.partial(exchange_kernel, lay),
        name="exchange",
        out_shape=(jax.ShapeDtypeStruct((block_rows, 4 * width), BF16), jax.ShapeDtypeStruct(pieces, F32)),
        in_specs=[VMEM] * 6 + [SMEM],
        out_specs=(pl.BlockSpec(memory_space=pl.ANY), pl.BlockSpec(memory_space=pl.ANY)),
        scratch_shapes=[
            pltpu.VMEM((block_rows, 4 * width), BF16),
            pltpu.VMEM((4, rim, width), BF16),
            pltpu.VMEM((2, first + second, width), F32),
            pltpu.VMEM((2, width, width), F32),
            pltpu.VMEM((width, width), F32),
            pltpu.VMEM((first, width), F32),
            pltpu.VMEM((second, width), F32),
            pltpu.VMEM((first, width), F32),
            pltpu.VMEM((second, width), F32),
            pltpu.VMEM((depth - 1, lay.chunks[0], width), F32),
            pltpu.VMEM((depth - 1, lay.chunks[1], width), F32),
            pltpu.VMEM(pieces, F32),
            pltpu.SemaphoreType.DMA((copies,)),
            pltpu.SemaphoreType.DMA((copies,)),
            pltpu.SemaphoreType.DMA((2,)),
        ],
        compiler_params=pltpu.CompilerParams(collective_id=0, has_side_effects=True, vmem_limit_bytes=LIMIT),
        cost_estimate=pl.CostEstimate(flops=4 * block_rows * width * width, bytes_accessed=2**23, transcendentals=0),
    )(base, rims, top, bottom, lower, upper, pick)


def whole_gram(pieces, second_rows):
    first = pieces.shape[3] - second_rows
    width = pieces.shape[-1]
    quarter, half = width // 4, width // 2
    grid = [[None] * 4 for _ in range(4)]
    for x in range(2):
        one, two = (
            (pieces[x, c, 1, quarter : 3 * quarter, :], pieces[x, c, :, first : first + half, :].reshape(width, width))
            for c in range(2)
        )
        side = jnp.concatenate([one[0], two[0]])
        grid[2 * x][2 * x + 1], grid[2 * x + 1][2 * x] = side, side.T
        for c, (_, cross) in enumerate((one, two)):
            grid[c][2 + x], grid[2 + x][c] = cross, cross.T
            grid[2 * x + c][2 * x + c] = jnp.concatenate([pieces[x, c, 0, : 3 * quarter], pieces[x, c, 1, :quarter]])
    return jnp.block(grid)


def shards(snapshots, mass_diag, lower_coupling, upper_coupling, band_offsets, start_basis):
    block_rows, width = snapshots.shape
    rim_rows = lower_coupling.shape[1]
    devices = lax.axis_size("rows")
    lay = Layout(devices, width)
    second_rows = lay.halves[1]
    row_index, group_index = lax.axis_index("rows"), lax.axis_index("groups")
    below, above = band_offsets[0, 0], band_offsets[0, 1]
    pick = jnp.stack(
        [(below == by) & (row_index - by >= 0) for by in (1, 2)] + [(above == by) & (row_index + by < devices) for by in (1, 2)]
    ).astype(F32)
    top, bottom = snapshots[:rim_rows, :], snapshots[block_rows - rim_rows :, :]
    base = (mass_diag[:, None] * snapshots.astype(F32)).astype(BF16)
    rims = jnp.concatenate(
        [
            mass_diag[:rim_rows, None] * top.astype(F32),
            mass_diag[block_rows - rim_rows :, None] * bottom.astype(F32),
        ]
    )
    gathered, pieces = exchange(lay, base, rims, top, bottom, lower_coupling[0], upper_coupling[0], pick)
    part_modes = start_basis.shape[1] // lax.axis_size("groups")
    high, low, start_ok = prepare_start(start_basis)
    basis_part, iterate_ok = iterate(group_index.reshape(1), part_modes, second_rows, pieces, high, low)
    basis_part = lax.cond(
        (start_ok[0] > 0) & (iterate_ok[0] > 0),
        lambda *_: basis_part,
        lambda pieces, start: direct_part(group_index, part_modes, whole_gram(pieces, second_rows), start),
        pieces,
        start_basis,
    )
    return lax.dot_general(gathered, basis_part, (((1,), (1,)), ((), ())), preferred_element_type=F32)


def solution(mesh):
    placed = (
        P("rows", "groups"),
        P("rows"),
        P("rows", None, None),
        P("rows", None, None),
        P("rows", None),
        P(),
    )
    return jax.shard_map(
        shards, mesh=mesh, in_specs=placed, out_specs=P("rows", "groups"), check_vma=False
    )
```
